256 devices in a mesh: dp: 4 (over y_hi, core), expert: 64 (over x, z, y_lo).
Axes of the slice: x: 4, y: 4 (y_hi: 2, y_lo: 2; y = y_hi * 2 + y_lo), z: 8, core: 2. Of those that a mesh axis runs over, the one named last changes fastest.
Arguments:
- tokens: bfloat16 [2, 1024, 6144], P(None, ('dp', 'expert')), may hold values from -6 to 6
- cotangent: bfloat16 [2, 1024, 6144], P(None, ('dp', 'expert')), may hold values from -6 to 6
- expert_ids: int32 [2, 1024, 2], P(None, ('dp', 'expert')), may hold values from 0 to 7, as said below
- gates: float32 [2, 1024], P(None, ('dp', 'expert')), may hold values from 0.2 to 1
- gate_weight: bfloat16 [6144, 16384], P('dp', 'expert'), may hold values from -0.078125 to 0.078125
- up_weight: bfloat16 [6144, 16384], P('dp', 'expert'), may hold values from -0.078125 to 0.078125
- down_weight: bfloat16 [16384, 6144], P('expert', 'dp'), may hold values from -0.046875 to 0.046875
Outputs:
- mixed: bfloat16 [2, 1024, 6144], P(None, ('dp', 'expert'))
- grad_gate: float32 [6144, 16384], P('dp', 'expert')
- grad_up: float32 [6144, 16384], P('dp', 'expert')
- grad_down: float32 [16384, 6144], P('expert', 'dp')
The draws below stay inside these ranges and needn't reach their ends.
Inputs may be any that keep to these rules, and one draw needn't show every extreme that they name: `expert_ids`: in each micro-batch at most 2 of the 4 tokens of one device name expert 0, and on at least one device exactly 2; a token's ids differ from each other.
All inputs are finite; a program needn't handle non-finite values.
Results may differ from the reference program's by a relative error of at most 0.022.
Values may be sent and summed in bfloat16 or wider, within the bound.
No kernel may reach another device: no remote copies, remote signals or barrier semaphores. Data moves between devices by JAX's collectives and lax.ppermute only.
A program may use at most 128 MiB of HBM per device.

```python
import jax
import jax.numpy as jnp
from jax import lax

D = 6144
FF = 16384
EXPERTS = 8
TOP = 2
MB = 2
TOK_DEV = 4
CAP = 2
TOKENS = 1024
N_DP = 4
N_EXPERT = 64


def draw_expert_ids(key, part):
    key = jax.random.fold_in(key, 7)
    keys = jax.random.split(key, 6)
    blocks = TOKENS // TOK_DEV
    counts = jax.random.randint(keys[0], (MB, blocks), 0, CAP + 1)
    chosen = jax.random.randint(keys[1], (MB, 1), 0, blocks)
    counts = jnp.where(jnp.arange(blocks)[None, :] == chosen, CAP, counts)
    scores = jax.random.randint(keys[2], (MB, blocks, TOK_DEV), 0, 1048576) * TOK_DEV + jnp.arange(TOK_DEV)[None, None, :]
    order_rank = jnp.argsort(jnp.argsort(scores, axis=-1), axis=-1)
    routed = order_rank < counts[..., None]
    column = jax.random.randint(keys[3], (MB, blocks, TOK_DEV), 0, 2)
    first_id = jax.random.randint(keys[4], (MB, blocks, TOK_DEV), 1, EXPERTS)
    id_shift = jax.random.randint(keys[5], (MB, blocks, TOK_DEV), 1, EXPERTS - 1)
    second = 1 + (first_id - 1 + id_shift) % (EXPERTS - 1)
    left_id = jnp.where(routed, jnp.where(column == 0, 0, first_id), first_id)
    right_id = jnp.where(routed, jnp.where(column == 0, first_id, 0), second)
    stacked = jnp.stack([left_id, right_id], axis=-1)
    return stacked.reshape(MB, TOKENS, TOP).astype(jnp.int32)


def level_of(key, dims, cuts, low, largest):
    def one(dim, parts):
        draws = jax.random.uniform(jax.random.fold_in(jax.random.fold_in(key, 6), dim), (parts,), jnp.float32, low / len(cuts), largest / len(cuts))
        return jnp.repeat(jnp.exp(draws), dims[dim] // parts).reshape((-1,) + (1,) * (len(dims) - dim - 1))

    gain = one(*cuts[0])
    for cut in cuts[1:]:
        gain = gain * one(*cut)
    return gain


def normal_values(stream_key, shape, width, most, cuts=(), kind=jnp.bfloat16):
    factor_of = level_of(stream_key, shape, cuts, -0.22, 0.18) if cuts else 1.0
    result = jax.random.normal(stream_key, shape, jnp.float32) * width * factor_of
    return jnp.minimum(jnp.maximum(result, -most), most).astype(kind)


def setup_inputs(seed: int = 0) -> dict:
    seeds = jax.random.split(jax.random.key(seed), 8)
    return {
        "tokens": normal_values(seeds[0], (MB, TOKENS, D), 1.0, 6.0, ((1, 256),)),
        "cotangent": normal_values(seeds[1], (MB, TOKENS, D), 1.0, 6.0, ((1, 256),)),
        "expert_ids": draw_expert_ids(jax.random.fold_in(seeds[7], 71), 0),
        "gates": jnp.clip(0.2 + 0.8 * jax.random.uniform(seeds[3], (MB, TOKENS), jnp.float32) ** level_of(seeds[3], (MB, TOKENS), ((1, 256),), -0.2, 0.2), 0.2, 1.0),
        "gate_weight": normal_values(seeds[4], (D, FF), D ** -0.5, 0.078125, ((0, 4), (1, 64))),
        "up_weight": normal_values(seeds[5], (D, FF), D ** -0.5, 0.078125, ((0, 4), (1, 64))),
        "down_weight": normal_values(seeds[6], (FF, D), FF ** -0.5, 0.046875, ((0, 64), (1, 4))),
    }


def silu_parts(gate_act):
    sigma = jax.nn.sigmoid(gate_act)
    return gate_act * sigma, sigma * (1.0 + gate_act * (1.0 - sigma))


def slot_map(expert_ids, slot_count):
    routed = jnp.any(expert_ids == 0, axis=-1).astype(jnp.int32)
    number = jnp.cumsum(routed, axis=-1, dtype=jnp.int32) - 1
    slots = jnp.arange(slot_count, dtype=jnp.int32)
    matched = (number[..., None, :] == slots[:, None]) & (routed[..., None, :] == 1)
    return matched.astype(jnp.float32)


def rounded(value):
    return lax.optimization_barrier(value.astype(jnp.bfloat16)).astype(jnp.float32)


def reference(tokens, cotangent, expert_ids, gates, gate_weight, up_weight, down_weight):
    block_shape = (MB, N_DP, N_EXPERT, TOK_DEV)
    select_map = slot_map(expert_ids.reshape(block_shape + (TOP,)), CAP)
    scaled = (gates[..., None] * cotangent.astype(jnp.float32)).astype(jnp.bfloat16)
    token_blocks = tokens.reshape(block_shape + (D,)).astype(jnp.float32)
    scaled_blocks = scaled.reshape(block_shape + (D,)).astype(jnp.float32)
    expert_rows = jnp.einsum("mpekt,mpetd->mpekd", select_map, token_blocks, precision=lax.Precision.HIGHEST).astype(jnp.bfloat16)
    cot_rows = jnp.einsum("mpekt,mpetd->mpekd", select_map, scaled_blocks, precision=lax.Precision.HIGHEST).astype(jnp.bfloat16)
    group_rows = MB * N_EXPERT * CAP
    grouped_x = jnp.transpose(expert_rows, (1, 0, 2, 3, 4)).reshape(N_DP, group_rows, D)
    grouped_c = jnp.transpose(cot_rows, (1, 0, 2, 3, 4)).reshape(N_DP, group_rows, D)

    def quarter(carry, pieces):
        rows_x, rows_c = pieces
        gate_act = jnp.dot(rows_x, gate_weight, preferred_element_type=jnp.float32)
        up_act = jnp.dot(rows_x, up_weight, preferred_element_type=jnp.float32)
        silu_act, slope = silu_parts(gate_act)
        hidden = (silu_act * up_act).astype(jnp.bfloat16)
        expert_out = jnp.dot(hidden, down_weight, preferred_element_type=jnp.float32)
        back_grad = lax.dot_general(rows_c, down_weight, (((1,), (1,)), ((), ())), preferred_element_type=jnp.float32)
        slope_gate = (back_grad * up_act * slope).astype(jnp.bfloat16)
        slope_up = (back_grad * silu_act).astype(jnp.bfloat16)
        term_gate = lax.dot_general(rows_x, slope_gate, (((0,), (0,)), ((), ())), preferred_element_type=jnp.float32)
        term_up = lax.dot_general(rows_x, slope_up, (((0,), (0,)), ((), ())), preferred_element_type=jnp.float32)
        term_down = lax.dot_general(hidden, rows_c, (((0,), (0,)), ((), ())), preferred_element_type=jnp.float32)
        updated = (carry[0] + rounded(term_gate), carry[1] + rounded(term_up), carry[2] + rounded(term_down))
        return updated, expert_out

    initial = (jnp.zeros((D, FF), jnp.float32), jnp.zeros((D, FF), jnp.float32), jnp.zeros((FF, D), jnp.float32))
    totals, outputs = lax.scan(quarter, initial, (grouped_x, grouped_c))
    outputs = jnp.transpose(outputs.reshape(N_DP, MB, N_EXPERT, CAP, D), (1, 0, 2, 3, 4))
    token_out = jnp.einsum("mpekt,mpekd->mpetd", select_map, outputs, precision=lax.Precision.HIGHEST)
    mixed = (gates.reshape(block_shape)[..., None] * token_out).reshape(MB, TOKENS, D).astype(jnp.bfloat16)
    return mixed, totals[0], totals[1], totals[2]
```

```python
import jax
import jax.numpy as jnp
from jax import lax
from jax.sharding import Mesh
from jax.sharding import PartitionSpec as P

SIZES = {"y_hi": 2, "core": 2, "x": 4, "z": 8, "y_lo": 2}
NAMES = tuple(SIZES)
DP = ("y_hi", "core")
EXPERT = ("x", "z", "y_lo")
Y_GROUP = ("y_hi", "core", "y_lo")
HALF = jnp.bfloat16


def shifted(value, axis, step):
    count = SIZES[axis]
    return lax.ppermute(value, axis, [(i, (i + step) % count) for i in range(count)])


def ring_gather(own, axis):
    count = SIZES[axis]
    pieces = [None] * count
    pieces[0] = own
    ahead = behind = own
    for step in range(1, count // 2):
        behind = shifted(behind, axis, 1)
        ahead = shifted(ahead, axis, -1)
        pieces[count - step] = behind
        pieces[step] = ahead
    cut = own.shape[0] // 2
    pieces[count // 2] = jnp.concatenate(
        [shifted(behind[:cut], axis, 1), shifted(ahead[cut:], axis, -1)], axis=0
    )
    return pieces


def send_home(pieces, axis):
    total = pieces[0].astype(jnp.float32)
    arrived = [shifted(pieces[d].astype(HALF), axis, d) for d in range(1, SIZES[axis])]
    for piece in arrived:
        total = total + piece.astype(jnp.float32)
    return total


def dot(a, b, a_dim, b_dim):
    return lax.dot_general(
        a, b, (((a_dim,), (b_dim,)), ((), ())), preferred_element_type=jnp.float32
    )


def exchange_sum(value, axis):
    me = lax.axis_index(axis)
    mine = jnp.where(me == 0, value[0], value[1])
    other = jnp.where(me == 0, value[1], value[0]).astype(HALF)
    return mine + shifted(other, axis, 1).astype(jnp.float32)


def exchange_join(value, axis):
    me = lax.axis_index(axis)
    other = shifted(value, axis, 1)
    return jnp.where(me == 0, jnp.stack([value, other]), jnp.stack([other, value]))


def slot_map(expert_ids, slot_count):
    routed = jnp.any(expert_ids == 0, axis=-1).astype(jnp.int32)
    number = jnp.cumsum(routed, axis=-1, dtype=jnp.int32) - 1
    slots = jnp.arange(slot_count, dtype=jnp.int32)
    matched = (number[:, None, :] == slots[:, None]) & (routed[:, None, :] == 1)
    return matched.astype(jnp.float32)


def shards(tokens, cotangent, expert_ids, gates, gate_weight, up_weight, down_weight):
    micro_count, tok_dev, model_width = tokens.shape
    slot_count = tok_dev // 2
    rows_dev = micro_count * slot_count
    width_dev, hidden_dev = gate_weight.shape
    n_dp = model_width // width_dev
    n_x, n_z, n_y = SIZES["x"], SIZES["z"], 2 * n_dp
    unit = n_y * rows_dev

    select = slot_map(expert_ids, slot_count)
    scaled = (gates[..., None] * cotangent.astype(jnp.float32)).astype(HALF)

    def compact(values):
        return jnp.sum(
            select[..., None] * values[:, None].astype(jnp.float32), axis=2
        ).astype(HALF)

    own = jnp.stack([compact(tokens), compact(scaled)]).reshape(2, rows_dev, n_dp, 1, width_dev)
    own = jnp.transpose(own, (2, 3, 0, 1, 4))
    own = jnp.broadcast_to(own, (n_dp, 2, 2, rows_dev, width_dev))
    own = own.reshape(n_y, 2, rows_dev, width_dev)
    got = lax.all_to_all(own, Y_GROUP, 0, 0)
    unit_x = got[:, 0].reshape(unit, width_dev)
    unit_c = got[:, 1].reshape(unit, width_dev)

    rows_x = jnp.concatenate(ring_gather(unit_x, "z"), axis=0)
    rows_x = ring_gather(rows_x, "x")
    rows_c = jnp.concatenate(ring_gather(unit_c, "x"), axis=0)
    rows_c = ring_gather(rows_c, "z")

    weight = jnp.concatenate([gate_weight, up_weight], axis=1)
    first = jnp.stack([dot(piece, weight, 1, 0) for piece in rows_x])
    back = jnp.stack([dot(piece, down_weight, 1, 1) for piece in rows_c])
    back = jnp.swapaxes(back.reshape(n_z, n_x, unit, hidden_dev), 0, 1)
    partial = jnp.concatenate(
        [first.reshape(n_x, n_z * unit, 2 * hidden_dev), back.reshape(n_x, n_z * unit, hidden_dev)],
        axis=-1,
    )
    partial = partial.reshape(2, 2, n_z * unit, 3 * hidden_dev)
    quarter = exchange_sum(jnp.swapaxes(partial, 0, 1), "core")
    quarter = exchange_sum(quarter, "y_hi")

    gate_act = quarter[:, :hidden_dev]
    up_act = quarter[:, hidden_dev : 2 * hidden_dev]
    back_act = quarter[:, 2 * hidden_dev :]
    sigma = jax.nn.sigmoid(gate_act)
    silu_act = gate_act * sigma
    hidden = silu_act * up_act
    slope_gate = back_act * up_act * (sigma * (1.0 + gate_act * (1.0 - sigma)))
    slope_up = back_act * silu_act
    acts = jnp.concatenate([slope_gate, slope_up, hidden], axis=-1).astype(HALF)
    acts = exchange_join(exchange_join(acts, "y_hi"), "core")
    acts = jnp.swapaxes(acts, 0, 1).reshape(n_x, n_z, unit, 3 * hidden_dev)
    slopes = acts[..., : 2 * hidden_dev].reshape(-1, 2 * hidden_dev)
    hidden = acts[..., 2 * hidden_dev :]

    cut = width_dev * 2 // 3
    out = dot(hidden.reshape(-1, hidden_dev), down_weight, 1, 0).astype(HALF)
    out = out.reshape(n_x, n_z, unit, width_dev)
    out_a, out_b = out[..., :cut], out[..., cut:]
    out_a = send_home([out_a[d] for d in range(n_x)], "x")
    out_a = send_home([out_a[d] for d in range(n_z)], "z")
    out_b = send_home([out_b[:, d] for d in range(n_z)], "z")
    out_b = send_home([out_b[d] for d in range(n_x)], "x")
    out = jnp.concatenate([out_a, out_b], axis=-1).reshape(n_y, rows_dev, width_dev)

    full_x = jnp.concatenate(rows_x, axis=0)
    full_c = jnp.concatenate(rows_c, axis=0)
    grads = dot(full_x, slopes, 0, 0)
    grad_gate, grad_up = grads[:, :hidden_dev], grads[:, hidden_dev:]
    hidden_c = jnp.swapaxes(hidden, 0, 1).reshape(-1, hidden_dev)
    grad_down = dot(hidden_c, full_c, 0, 0)

    got = lax.all_to_all(out, Y_GROUP, 0, 0).reshape(n_dp, 2, rows_dev, width_dev)
    slot_out = jnp.transpose(got[:, 0] + got[:, 1], (1, 0, 2))
    slot_out = slot_out.reshape(micro_count, slot_count, 1, model_width)
    token_out = jnp.sum(select[..., None] * slot_out, axis=1)
    mixed = (gates[..., None] * token_out).astype(HALF)
    return (mixed, grad_gate, grad_up, grad_down)


def solution(mesh):
    fine = Mesh(mesh.devices.reshape(tuple(SIZES.values())), NAMES)
    tokens = DP + EXPERT
    return jax.shard_map(
        shards,
        mesh=fine,
        in_specs=(
            P(None, tokens, None),
            P(None, tokens, None),
            P(None, tokens, None),
            P(None, tokens),
            P(DP, EXPERT),
            P(DP, EXPERT),
            P(EXPERT, DP),
        ),
        out_specs=(
            P(None, tokens, None),
            P(DP, EXPERT),
            P(DP, EXPERT),
            P(EXPERT, DP),
        ),
        check_vma=False,
    )
```

```python
import jax
import jax.numpy as jnp
from jax import lax
from jax.sharding import Mesh
from jax.sharding import PartitionSpec as P

SIZES = {"y_hi": 2, "core": 2, "x": 4, "z": 8, "y_lo": 2}
NAMES = tuple(SIZES)
DP = ("y_hi", "core")
EXPERT = ("x", "z", "y_lo")
XY_GROUP = ("y_hi", "core", "x", "y_lo")
Y_GROUP = ("y_hi", "core", "y_lo")
Y_RING = ("y_hi", "y_lo")
HALF = jnp.bfloat16
barrier = lax.optimization_barrier


def shifted(value, axis, step):
    count = 4 if axis == Y_RING else SIZES[axis]
    return lax.ppermute(value, axis, [(i, (i + step) % count) for i in range(count)])


def traded(value):
    return lax.ppermute(value, ("core", "y_lo"), [(0, 0), (1, 2), (2, 1), (3, 3)])


def picked(value, axis):
    me = lax.axis_index(axis)
    return jnp.where(me == 0, value[0], value[1]), jnp.where(me == 0, value[1], value[0])


def send_home(pieces, axis):
    arrived = [shifted(pieces[d], axis, d) for d in (2, 1, 3)]
    total = pieces[0].astype(jnp.float32)
    for piece in arrived:
        total = total + piece.astype(jnp.float32)
    return total


def dot(a, b, a_dim, b_dim):
    return lax.dot_general(
        a, b, (((a_dim,), (b_dim,)), ((), ())), preferred_element_type=jnp.float32
    )


def natural(pair):
    return jnp.stack(picked(jnp.stack([part.astype(HALF) for part in pair]), "core"))


def ring_sum(partial):
    rows = partial.shape[0] // 4
    me = lax.axis_index(Y_RING)

    def quarter(step):
        return lax.dynamic_slice_in_dim(partial, ((me + step) & 3) * rows, rows, axis=0)

    arrived = [shifted(quarter(step), Y_RING, step) for step in (2, 1, 3)]
    total = quarter(0).astype(jnp.float32)
    for piece in arrived:
        total = total + piece.astype(jnp.float32)
    return total


def ring_join(own):
    opposite, behind, ahead = [shifted(own, Y_RING, step) for step in (2, 1, 3)]
    return jnp.concatenate([own, ahead, opposite, behind], axis=0)


def row_maps(rows):
    me, x, z = (lax.axis_index(axis) for axis in (Y_RING, "x", "z"))
    row = jnp.arange(rows, dtype=jnp.int32)

    def place(gathered):
        return ((gathered // 256 - me) & 3) * 256 + gathered % 256

    distance = (row // 8 - z) & 7
    slot = jnp.where(
        distance == 0, 0, jnp.where(distance <= 4, 2 * distance - 1, 2 * (8 - distance))
    )
    owner_x = (row // 256 + x) & 3
    gathered = slot * 128 + (row // 64 & 3) * 32 + owner_x * 8 + row % 8
    places = barrier((place(row), place(gathered)))
    joined = lax.broadcasted_iota(jnp.int32, (rows, rows), 1)
    return [(joined == place[:, None]).astype(HALF) for place in places]


def next_round(pieces, last):
    if not last:
        return [shifted(pieces[-2], "z", -1), shifted(pieces[-1], "z", 1)]
    cut = pieces[0].shape[0] // 2
    return [shifted(pieces[-1][:cut], "z", 1), shifted(pieces[-2][cut:], "z", -1)]


def slot_map(expert_ids, slot_count):
    routed = jnp.any(expert_ids == 0, axis=-1).astype(jnp.int32)
    number = jnp.cumsum(routed, axis=-1, dtype=jnp.int32) - 1
    slots = jnp.arange(slot_count, dtype=jnp.int32)
    matched = (number[:, None, :] == slots[:, None]) & (routed[:, None, :] == 1)
    return matched.astype(jnp.float32)


def shards(tokens, cotangent, expert_ids, gates, gate_weight, up_weight, down_weight):
    micro_count, tok_dev, model_width = tokens.shape
    slot_count = tok_dev // 2
    rows_dev = micro_count * slot_count
    width_dev, hidden_dev = gate_weight.shape
    half = width_dev // 2
    n_x, n_z = SIZES["x"], SIZES["z"]

    select = slot_map(expert_ids, slot_count)

    def compact(values):
        own = jnp.sum(select[..., None] * values[:, None].astype(jnp.float32), axis=2)
        return own.astype(HALF).reshape(rows_dev, 2, 2, 2, half)

    scaled = (gates[..., None] * cotangent.astype(jnp.float32)).astype(HALF)
    own = jnp.stack([compact(tokens), compact(scaled)])
    own = jnp.transpose(own, (2, 4, 3, 0, 1, 5))[:, :, None]
    own = jnp.broadcast_to(own, (2, 2, n_x, 2, 2, rows_dev, half))
    got = lax.all_to_all(own.reshape(-1, 2, rows_dev, half), XY_GROUP, 0, 0)

    weight = jnp.concatenate([gate_weight, up_weight, down_weight.T], axis=1)
    weight = jnp.stack(picked(weight.reshape(2, half, 3 * hidden_dev), "y_lo"))
    maps = row_maps(n_x * n_z * 32)
    got, weight, maps = barrier((got, weight, maps))
    to_gathered, to_owners = maps
    weight = traded(weight)

    x_unit, c_unit = got[:, 0].reshape(-1, half), got[:, 1].reshape(-1, half)
    x_pieces = [x_unit, x_unit]
    for step in range(n_z // 2):
        x_pieces = x_pieces + next_round(x_pieces, step == n_z // 2 - 1)
    x_own = jnp.concatenate(x_pieces[1:], axis=0)
    x_own, c_unit, weight = barrier((x_own, c_unit, weight))
    gate_up = weight[:, :, : 2 * hidden_dev]

    x_other = shifted(x_own, "core", 1)
    partial = dot(x_own, gate_up[0], 1, 0) + dot(x_other, gate_up[1], 1, 0)
    c_pieces = next_round([c_unit, c_unit], False)
    partial, c_pieces = barrier((partial.astype(HALF), c_pieces))
    down = jnp.swapaxes(weight[:, :, 2 * hidden_dev :], 1, 2)

    acts = ring_sum(partial)
    c_pieces = [c_unit] + c_pieces
    for _ in range(n_z // 2 - 2):
        c_pieces = c_pieces + next_round(c_pieces, False)
    acts, c_pieces, down = barrier((acts, c_pieces, down))

    gate_act, up_act = acts[:, :hidden_dev], acts[:, hidden_dev:]
    sigma = jax.nn.sigmoid(gate_act)
    silu_act = gate_act * sigma
    slope = sigma * (1.0 + gate_act * (1.0 - sigma))
    hidden = ring_join((silu_act * up_act).astype(HALF))
    c_pieces = c_pieces + next_round(c_pieces, True)
    hidden, c_pieces = barrier((hidden, c_pieces))
    c_own = jnp.concatenate(c_pieces, axis=0)

    placed = dot(to_owners, hidden, 1, 0).astype(HALF)
    out = shifted(dot(placed, down[1], 1, 0).astype(HALF), "core", 1)
    out = dot(placed, down[0], 1, 0) + out.astype(jnp.float32)
    c_other = shifted(c_own, "core", 1)
    back = dot(c_own, down[0], 1, 1) + dot(c_other, down[1], 1, 1)
    out, back = barrier((out.astype(HALF), back.astype(HALF)))

    out = send_home(out.reshape(n_x, -1, half), "x").astype(HALF)
    back_act = ring_sum(back)
    slopes = jnp.concatenate([back_act * up_act * slope, back_act * silu_act], axis=-1)
    slopes, hidden, c_own = barrier((slopes.astype(HALF), hidden, c_own))
    slopes = ring_join(slopes)
    hidden = dot(to_gathered, hidden, 1, 0).astype(HALF)
    down_pair = natural([dot(hidden, rows, 0, 0) for rows in (c_own, c_other)])
    down_pair = traded(down_pair)
    out, slopes = barrier((out, slopes))

    out = jnp.transpose(out.reshape(4, n_z, 2, rows_dev, half), (1, 0, 2, 3, 4))
    out = lax.all_to_all(out.reshape(n_z, 8, rows_dev, half), "z", 0, 0)
    out = jnp.sum(out.astype(jnp.float32), axis=0)
    slopes = dot(to_gathered, slopes, 1, 0).astype(HALF)
    pair = natural([dot(rows, slopes, 0, 0) for rows in (x_own, x_other)])
    pair = jnp.stack([pair[..., :hidden_dev], pair[..., hidden_dev:]])
    pair = traded(pair).astype(jnp.float32)
    grad_gate, grad_up = pair.reshape(2, width_dev, hidden_dev)
    grad_down = jnp.concatenate([down_pair[0], down_pair[1]], axis=1).astype(jnp.float32)
    got = lax.all_to_all(out, Y_GROUP, 0, 0).reshape(2, 2, 2, rows_dev, half)
    slot_out = jnp.transpose(got, (3, 0, 2, 1, 4))
    slot_out = slot_out.reshape(micro_count, slot_count, 1, model_width)
    token_out = jnp.sum(select[..., None] * slot_out, axis=1)
    mixed = (gates[..., None] * token_out).astype(HALF)

    return (mixed, grad_gate, grad_up, grad_down)


def solution(mesh):
    fine = Mesh(mesh.devices.reshape(tuple(SIZES.values())), NAMES)
    tokens = DP + EXPERT
    return jax.shard_map(
        shards,
        mesh=fine,
        in_specs=(
            P(None, tokens, None),
            P(None, tokens, None),
            P(None, tokens, None),
            P(None, tokens),
            P(DP, EXPERT),
            P(DP, EXPERT),
            P(EXPERT, DP),
        ),
        out_specs=(
            P(None, tokens, None),
            P(DP, EXPERT),
            P(DP, EXPERT),
            P(EXPERT, DP),
        ),
        check_vma=False,
    )
```

```python
import jax
import jax.numpy as jnp
from jax import lax
from jax.sharding import Mesh
from jax.sharding import PartitionSpec as P

SIZES = {"y_hi": 2, "core": 2, "x": 4, "z": 8, "y_lo": 2}
NAMES = tuple(SIZES)
DP = ("y_hi", "core")
EXPERT = ("x", "z", "y_lo")
XY_GROUP = ("y_hi", "core", "x", "y_lo")
YZ_GROUP = ("y_hi", "core", "z", "y_lo")
Y_RING = ("y_hi", "y_lo")
HALF = jnp.bfloat16
barrier = lax.optimization_barrier


def shifted(value, axis, step):
    count = 4 if axis == Y_RING else SIZES[axis]
    return lax.ppermute(value, axis, [(i, (i + step) % count) for i in range(count)])


def traded(value):
    return lax.ppermute(value, ("core", "y_lo"), [(0, 0), (1, 2), (2, 1), (3, 3)])


def picked(value, axis):
    me = lax.axis_index(axis)
    return jnp.where(me == 0, value[0], value[1]), jnp.where(me == 0, value[1], value[0])


def send_home(pieces, axis):
    arrived = [shifted(pieces[d], axis, d) for d in (2, 1, 3)]
    total = pieces[0].astype(jnp.float32)
    for piece in arrived:
        total = total + piece.astype(jnp.float32)
    return total


def dot(a, b, a_dim, b_dim):
    return lax.dot_general(
        a, b, (((a_dim,), (b_dim,)), ((), ())), preferred_element_type=jnp.float32
    )


def products(pair, acts):
    return jnp.stack([dot(rows, acts, 0, 0).astype(HALF) for rows in pair])


def ring_sum(partial):
    rows = partial.shape[0] // 4
    me = lax.axis_index(Y_RING)

    def quarter(step):
        return lax.dynamic_slice_in_dim(partial, ((me + step) & 3) * rows, rows, axis=0)

    arrived = [shifted(quarter(step), Y_RING, step) for step in (2, 1, 3)]
    total = quarter(0).astype(jnp.float32)
    for piece in arrived:
        total = total + piece.astype(jnp.float32)
    return total


def ring_join(own):
    opposite, behind, ahead = [shifted(own, Y_RING, step) for step in (2, 1, 3)]
    return [own, ahead, opposite, behind]


def row_maps(rows):
    me, x, z = (lax.axis_index(axis) for axis in (Y_RING, "x", "z"))
    row = jnp.arange(rows, dtype=jnp.int32)

    def place(gathered):
        return ((gathered // 256 - me) & 3) * 256 + gathered % 256

    distance = (row // 8 - z) & 7
    slot = jnp.where(
        distance == 0, 0, jnp.where(distance <= 4, 2 * distance - 1, 2 * (8 - distance))
    )
    owner_x = (row // 256 + x) & 3
    gathered = slot * 128 + (row // 64 & 3) * 32 + owner_x * 8 + row % 8
    places = barrier((place(row), place(gathered)))
    joined = lax.broadcasted_iota(jnp.int32, (rows, rows), 1)
    return [(joined == place[:, None]).astype(HALF) for place in places]


def next_round(pieces, last):
    if not last:
        return [shifted(pieces[-2], "z", -1), shifted(pieces[-1], "z", 1)]
    cut = pieces[0].shape[0] // 2
    return [shifted(pieces[-1][:cut], "z", 1), shifted(pieces[-2][cut:], "z", -1)]


def slot_map(expert_ids, slot_count):
    routed = jnp.any(expert_ids == 0, axis=-1).astype(jnp.int32)
    number = jnp.cumsum(routed, axis=-1, dtype=jnp.int32) - 1
    slots = jnp.arange(slot_count, dtype=jnp.int32)
    matched = (number[:, None, :] == slots[:, None]) & (routed[:, None, :] == 1)
    return matched.astype(jnp.float32)


def shards(tokens, cotangent, expert_ids, gates, gate_weight, up_weight, down_weight):
    micro_count, tok_dev, model_width = tokens.shape
    slot_count = tok_dev // 2
    rows_dev = micro_count * slot_count
    width_dev, hidden_dev = gate_weight.shape
    half = width_dev // 2
    n_x, n_z = SIZES["x"], SIZES["z"]

    select = slot_map(expert_ids, slot_count)

    def compact(values):
        own = jnp.sum(select[..., None] * values[:, None].astype(jnp.float32), axis=2)
        return own.astype(HALF).reshape(rows_dev, 2, 2, 2, half)

    scaled = (gates[..., None] * cotangent.astype(jnp.float32)).astype(HALF)
    own = jnp.stack([compact(tokens), compact(scaled)])
    own = jnp.transpose(own, (2, 4, 3, 0, 1, 5))[:, :, None]
    own = jnp.broadcast_to(own, (2, 2, n_x, 2, 2, rows_dev, half))
    got = lax.all_to_all(own.reshape(-1, 2, rows_dev, half), XY_GROUP, 0, 0)

    weight = jnp.concatenate([gate_weight, up_weight, down_weight.T], axis=1)
    weight = jnp.stack(picked(weight.reshape(2, half, 3 * hidden_dev), "y_lo"))
    maps = row_maps(n_x * n_z * 32)
    got, weight, maps = barrier((got, weight, maps))
    to_gathered, to_owners = maps
    weight = traded(weight)

    x_unit, c_unit = got[:, 0].reshape(-1, half), got[:, 1].reshape(-1, half)
    x_pieces = [x_unit, x_unit]
    for step in range(n_z // 2):
        x_pieces = x_pieces + next_round(x_pieces, step == n_z // 2 - 1)
    x_own = jnp.concatenate(x_pieces[1:], axis=0)
    x_own, c_unit, weight = barrier((x_own, c_unit, weight))
    gate_up = weight[:, :, : 2 * hidden_dev]

    x_other = shifted(x_own, "core", 1)
    partial = dot(x_own, gate_up[0], 1, 0) + dot(x_other, gate_up[1], 1, 0)
    c_pieces = next_round([c_unit, c_unit], False)
    partial, c_pieces = barrier((partial.astype(HALF), c_pieces))
    down = jnp.swapaxes(weight[:, :, 2 * hidden_dev :], 1, 2)

    acts = ring_sum(partial)
    c_pieces = [c_unit] + c_pieces
    for _ in range(n_z // 2 - 2):
        c_pieces = c_pieces + next_round(c_pieces, False)
    acts, c_pieces, down = barrier((acts, c_pieces, down))

    gate_act, up_act = acts[:, :hidden_dev], acts[:, hidden_dev:]
    sigma = jax.nn.sigmoid(gate_act)
    silu_act = gate_act * sigma
    slope = sigma * (1.0 + gate_act * (1.0 - sigma))
    hidden = jnp.concatenate(ring_join((silu_act * up_act).astype(HALF)), axis=0)
    c_pieces = c_pieces + next_round(c_pieces, True)
    hidden, c_pieces = barrier((hidden, c_pieces))
    c_own = jnp.concatenate(c_pieces, axis=0)

    placed = dot(to_owners, hidden, 1, 0).astype(HALF)
    out = shifted(dot(placed, down[1], 1, 0).astype(HALF), "core", 1)
    out = dot(placed, down[0], 1, 0) + out.astype(jnp.float32)
    c_other = shifted(c_own, "core", 1)
    back = dot(c_own, down[0], 1, 1) + dot(c_other, down[1], 1, 1)
    out, back = barrier((out.astype(HALF), back.astype(HALF)))

    out = send_home(out.reshape(n_x, -1, half), "x").astype(HALF)
    back_act = ring_sum(back)
    slopes = jnp.concatenate([back_act * up_act * slope, back_act * silu_act], axis=-1)
    slopes = ring_join(slopes.astype(HALF))
    early, hidden = barrier((slopes[1], hidden))
    slopes = jnp.concatenate([slopes[0], early] + slopes[2:], axis=0)
    hidden = dot(to_gathered, hidden, 1, 0).astype(HALF)
    down_pair = jnp.stack([dot(hidden, rows, 0, 0).astype(HALF) for rows in (c_own, c_other)])
    down_pair = traded(down_pair)
    slopes = dot(to_gathered, slopes, 1, 0).astype(HALF)
    pair = products((x_own, x_other), slopes)
    out, pair, down_pair = barrier((out, pair, down_pair))

    got = lax.all_to_all(out.reshape(-1, rows_dev, half), YZ_GROUP, 0, 0)
    pair = jnp.concatenate(picked(traded(pair), "y_lo"), axis=0)
    grad_gate = pair[:, :hidden_dev].astype(jnp.float32)
    grad_up = pair[:, hidden_dev:].astype(jnp.float32)
    got, grad_gate, grad_up = barrier((got, grad_gate, grad_up))
    got = jnp.sum(got.reshape(2, 2, n_z, 2, rows_dev, half).astype(jnp.float32), axis=2)
    grad_down = jnp.concatenate(picked(down_pair, "y_lo"), axis=1).astype(jnp.float32)
    slot_out = jnp.transpose(got, (3, 0, 2, 1, 4))
    slot_out = slot_out.reshape(micro_count, slot_count, 1, model_width)
    token_out = jnp.sum(select[..., None] * slot_out, axis=1)
    mixed = (gates[..., None] * token_out).astype(HALF)

    return (mixed, grad_gate, grad_up, grad_down)


def solution(mesh):
    fine = Mesh(mesh.devices.reshape(tuple(SIZES.values())), NAMES)
    tokens = DP + EXPERT
    return jax.shard_map(
        shards,
        mesh=fine,
        in_specs=(
            P(None, tokens, None),
            P(None, tokens, None),
            P(None, tokens, None),
            P(None, tokens),
            P(DP, EXPERT),
            P(DP, EXPERT),
            P(EXPERT, DP),
        ),
        out_specs=(
            P(None, tokens, None),
            P(DP, EXPERT),
            P(DP, EXPERT),
            P(EXPERT, DP),
        ),
        check_vma=False,
    )
```

```python
import jax
import jax.numpy as jnp
from jax import lax
from jax.sharding import Mesh
from jax.sharding import PartitionSpec as P

SIZES = {"y_hi": 2, "core": 2, "x": 4, "z": 8, "y_lo": 2}
NAMES = tuple(SIZES)
DP = ("y_hi", "core")
EXPERT = ("x", "z", "y_lo")
XY_GROUP = ("y_hi", "core", "x", "y_lo")
YZ_GROUP = ("y_hi", "core", "z", "y_lo")
Y_RING = ("y_hi", "y_lo")
HALF = jnp.bfloat16
barrier = lax.optimization_barrier


def shifted(value, axis, step):
    count = 4 if axis == Y_RING else SIZES[axis]
    return lax.ppermute(value, axis, [(i, (i + step) % count) for i in range(count)])


def traded(value):
    return lax.ppermute(value, ("core", "y_lo"), [(0, 0), (1, 2), (2, 1), (3, 3)])


def picked(value, axis):
    me = lax.axis_index(axis)
    return jnp.where(me == 0, value[0], value[1]), jnp.where(me == 0, value[1], value[0])


def send_home(pieces, axis):
    arrived = [shifted(pieces[d], axis, d) for d in (2, 1, 3)]
    total = pieces[0].astype(jnp.float32)
    for piece in arrived:
        total = total + piece.astype(jnp.float32)
    return total


def dot(a, b, a_dim, b_dim):
    return lax.dot_general(
        a, b, (((a_dim,), (b_dim,)), ((), ())), preferred_element_type=jnp.float32
    )


def products(pair, acts):
    return jnp.stack([dot(rows, acts, 0, 0).astype(HALF) for rows in pair])


def ring_sum(partial):
    rows = partial.shape[0] // 4
    me = lax.axis_index(Y_RING)

    def quarter(step):
        return lax.dynamic_slice_in_dim(partial, ((me + step) & 3) * rows, rows, axis=0)

    arrived = [shifted(quarter(step), Y_RING, step) for step in (2, 1, 3)]
    total = quarter(0).astype(jnp.float32)
    for piece in arrived:
        total = total + piece.astype(jnp.float32)
    return total


def ring_join(own):
    behind, ahead, opposite = [shifted(own, Y_RING, step) for step in (1, 3, 2)]
    return [own, ahead, opposite, behind]


def row_maps(rows):
    me, x, z = (lax.axis_index(axis) for axis in (Y_RING, "x", "z"))
    row = jnp.arange(rows, dtype=jnp.int32)

    def place(gathered):
        return ((gathered // 256 - me) & 3) * 256 + gathered % 256

    distance = (row // 8 - z) & 7
    slot = jnp.where(
        distance == 0, 0, jnp.where(distance <= 4, 2 * distance - 1, 2 * (8 - distance))
    )
    owner_x = (row // 256 + x) & 3
    gathered = slot * 128 + (row // 64 & 3) * 32 + owner_x * 8 + row % 8
    places = barrier((place(row), place(gathered)))
    joined = lax.broadcasted_iota(jnp.int32, (rows, rows), 1)
    return [(joined == place[:, None]).astype(HALF) for place in places]


def next_round(pieces, last):
    if not last:
        return [shifted(pieces[-2], "z", -1), shifted(pieces[-1], "z", 1)]
    cut = pieces[0].shape[0] // 2
    return [shifted(pieces[-1][:cut], "z", 1), shifted(pieces[-2][cut:], "z", -1)]


def slot_map(expert_ids, slot_count):
    routed = jnp.any(expert_ids == 0, axis=-1).astype(jnp.int32)
    number = jnp.cumsum(routed, axis=-1, dtype=jnp.int32) - 1
    slots = jnp.arange(slot_count, dtype=jnp.int32)
    matched = (number[:, None, :] == slots[:, None]) & (routed[:, None, :] == 1)
    return matched.astype(jnp.float32)


def shards(tokens, cotangent, expert_ids, gates, gate_weight, up_weight, down_weight):
    micro_count, tok_dev, model_width = tokens.shape
    slot_count = tok_dev // 2
    rows_dev = micro_count * slot_count
    width_dev, hidden_dev = gate_weight.shape
    half = width_dev // 2
    n_x, n_z = SIZES["x"], SIZES["z"]

    select = slot_map(expert_ids, slot_count)

    def compact(values):
        own = jnp.sum(select[..., None] * values[:, None].astype(jnp.float32), axis=2)
        return own.astype(HALF).reshape(rows_dev, 2, 2, 2, half)

    scaled = (gates[..., None] * cotangent.astype(jnp.float32)).astype(HALF)
    own = jnp.stack([compact(tokens), compact(scaled)])
    own = jnp.transpose(own, (2, 4, 3, 0, 1, 5))[:, :, None]
    own = jnp.broadcast_to(own, (2, 2, n_x, 2, 2, rows_dev, half))
    got = lax.all_to_all(own.reshape(-1, 2, rows_dev, half), XY_GROUP, 0, 0)

    weight = jnp.concatenate([gate_weight, up_weight, down_weight.T], axis=1)
    weight = jnp.stack(picked(weight.reshape(2, half, 3 * hidden_dev), "y_lo"))
    maps = row_maps(n_x * n_z * 32)
    got, weight, maps = barrier((got, weight, maps))
    to_gathered, to_owners = maps
    weight = traded(weight)

    x_unit, c_unit = got[:, 0].reshape(-1, half), got[:, 1].reshape(-1, half)
    x_pieces = [x_unit, x_unit]
    for step in range(n_z // 2):
        x_pieces = x_pieces + next_round(x_pieces, step == n_z // 2 - 1)
    x_own = jnp.concatenate(x_pieces[1:], axis=0)
    x_own, c_unit, weight = barrier((x_own, c_unit, weight))
    gate_up = weight[:, :, : 2 * hidden_dev]

    x_other = shifted(x_own, "core", 1)
    partial = dot(x_own, gate_up[0], 1, 0) + dot(x_other, gate_up[1], 1, 0)
    c_pieces = next_round([c_unit, c_unit], False)
    partial, c_pieces = barrier((partial.astype(HALF), c_pieces))
    down = jnp.swapaxes(weight[:, :, 2 * hidden_dev :], 1, 2)

    acts = ring_sum(partial)
    c_pieces = [c_unit] + c_pieces
    for _ in range(n_z // 2 - 2):
        c_pieces = c_pieces + next_round(c_pieces, False)
    acts, c_pieces, down = barrier((acts, c_pieces, down))

    gate_act, up_act = acts[:, :hidden_dev], acts[:, hidden_dev:]
    sigma = jax.nn.sigmoid(gate_act)
    silu_act = gate_act * sigma
    slope = sigma * (1.0 + gate_act * (1.0 - sigma))
    hidden = jnp.concatenate(ring_join((silu_act * up_act).astype(HALF)), axis=0)
    c_pieces = c_pieces + next_round(c_pieces, True)
    hidden, c_pieces = barrier((hidden, c_pieces))
    c_own = jnp.concatenate(c_pieces, axis=0)

    placed = dot(to_owners, hidden, 1, 0).astype(HALF)
    out = shifted(dot(placed, down[1], 1, 0).astype(HALF), "core", 1)
    out = dot(placed, down[0], 1, 0) + out.astype(jnp.float32)
    c_other = shifted(c_own, "core", 1)
    back = dot(c_own, down[0], 1, 1) + dot(c_other, down[1], 1, 1)
    out, back = barrier((out.astype(HALF), back.astype(HALF)))

    out = send_home(out.reshape(n_x, -1, half), "x").astype(HALF)
    back_act = ring_sum(back)
    slopes = jnp.concatenate([back_act * up_act * slope, back_act * silu_act], axis=-1)
    slopes = ring_join(slopes.astype(HALF))
    early, hidden = barrier((slopes[2], hidden))
    slopes = jnp.concatenate(slopes[:2] + [early, slopes[3]], axis=0)
    hidden = dot(to_gathered, hidden, 1, 0).astype(HALF)
    down_pair = jnp.stack([dot(hidden, rows, 0, 0).astype(HALF) for rows in (c_own, c_other)])
    down_pair = traded(down_pair)
    slopes = dot(to_gathered, slopes, 1, 0).astype(HALF)
    pair = products((x_own, x_other), slopes)
    out, pair, down_pair = barrier((out, pair, down_pair))

    got = lax.all_to_all(out.reshape(-1, rows_dev, half), YZ_GROUP, 0, 0)
    pair = jnp.concatenate(picked(traded(pair), "y_lo"), axis=0)
    grad_gate = pair[:, :hidden_dev].astype(jnp.float32)
    grad_up = pair[:, hidden_dev:].astype(jnp.float32)
    got, grad_gate, grad_up = barrier((got, grad_gate, grad_up))
    got = jnp.sum(got.reshape(2, 2, n_z, 2, rows_dev, half).astype(jnp.float32), axis=2)
    grad_down = jnp.concatenate(picked(down_pair, "y_lo"), axis=1).astype(jnp.float32)
    slot_out = jnp.transpose(got, (3, 0, 2, 1, 4))
    slot_out = slot_out.reshape(micro_count, slot_count, 1, model_width)
    token_out = jnp.sum(select[..., None] * slot_out, axis=1)
    mixed = (gates[..., None] * token_out).astype(HALF)

    return (mixed, grad_gate, grad_up, grad_down)


def solution(mesh):
    fine = Mesh(mesh.devices.reshape(tuple(SIZES.values())), NAMES)
    tokens = DP + EXPERT
    return jax.shard_map(
        shards,
        mesh=fine,
        in_specs=(
            P(None, tokens, None),
            P(None, tokens, None),
            P(None, tokens, None),
            P(None, tokens),
            P(DP, EXPERT),
            P(DP, EXPERT),
            P(EXPERT, DP),
        ),
        out_specs=(
            P(None, tokens, None),
            P(DP, EXPERT),
            P(DP, EXPERT),
            P(EXPERT, DP),
        ),
        check_vma=False,
    )
```

```python
import jax
import jax.numpy as jnp
from jax import lax
from jax.sharding import Mesh
from jax.sharding import PartitionSpec as P

SIZES = {"y_hi": 2, "core": 2, "x": 4, "z": 8, "y_lo": 2}
NAMES = tuple(SIZES)
DP = ("y_hi", "core")
EXPERT = ("x", "z", "y_lo")
XY_GROUP = ("y_hi", "core", "x", "y_lo")
YZ_GROUP = ("y_hi", "core", "z", "y_lo")
Y_RING = ("y_hi", "y_lo")
HALF = jnp.bfloat16
barrier = lax.optimization_barrier


def shifted(value, axis, step):
    count = 4 if axis == Y_RING else SIZES[axis]
    return lax.ppermute(value, axis, [(i, (i + step) % count) for i in range(count)])


def traded(value):
    return lax.ppermute(value, ("core", "y_lo"), [(0, 0), (1, 2), (2, 1), (3, 3)])


def picked(value, axis):
    me = lax.axis_index(axis)
    return jnp.where(me == 0, value[0], value[1]), jnp.where(me == 0, value[1], value[0])


def send_home(pieces, axis):
    arrived = [shifted(pieces[d], axis, d) for d in (2, 1, 3)]
    total = pieces[0].astype(jnp.float32)
    for piece in arrived:
        total = total + piece.astype(jnp.float32)
    return total


def dot(a, b, a_dim, b_dim):
    return lax.dot_general(
        a, b, (((a_dim,), (b_dim,)), ((), ())), preferred_element_type=jnp.float32
    )


def products(pair, acts):
    return jnp.stack([dot(rows, acts, 0, 0).astype(HALF) for rows in pair])


def ring_sum(partial):
    rows = partial.shape[0] // 4
    me = lax.axis_index(Y_RING)

    def quarter(step):
        return lax.dynamic_slice_in_dim(partial, ((me + step) & 3) * rows, rows, axis=0)

    arrived = [shifted(quarter(step), Y_RING, step) for step in (1, 3, 2)]
    total = quarter(0).astype(jnp.float32)
    for piece in arrived:
        total = total + piece.astype(jnp.float32)
    return total


def ring_join(own):
    behind, ahead, opposite = [shifted(own, Y_RING, step) for step in (1, 3, 2)]
    return [own, ahead, opposite, behind]


def row_maps(rows):
    me, x, z = (lax.axis_index(axis) for axis in (Y_RING, "x", "z"))
    row = jnp.arange(rows, dtype=jnp.int32)

    def place(gathered):
        return ((gathered // 256 - me) & 3) * 256 + gathered % 256

    distance = (row // 8 - z) & 7
    slot = jnp.where(
        distance == 0, 0, jnp.where(distance <= 4, 2 * distance - 1, 2 * (8 - distance))
    )
    owner_x = (row // 256 + x) & 3
    gathered = slot * 128 + (row // 64 & 3) * 32 + owner_x * 8 + row % 8
    places = barrier((place(row), place(gathered)))
    joined = lax.broadcasted_iota(jnp.int32, (rows, rows), 1)
    return [(joined == place[:, None]).astype(HALF) for place in places]


def next_round(pieces, last):
    if not last:
        return [shifted(pieces[-2], "z", -1), shifted(pieces[-1], "z", 1)]
    cut = pieces[0].shape[0] // 2
    return [shifted(pieces[-1][:cut], "z", 1), shifted(pieces[-2][cut:], "z", -1)]


def slot_map(expert_ids, slot_count):
    routed = jnp.any(expert_ids == 0, axis=-1).astype(jnp.int32)
    number = jnp.cumsum(routed, axis=-1, dtype=jnp.int32) - 1
    slots = jnp.arange(slot_count, dtype=jnp.int32)
    matched = (number[:, None, :] == slots[:, None]) & (routed[:, None, :] == 1)
    return matched.astype(jnp.float32)


def shards(tokens, cotangent, expert_ids, gates, gate_weight, up_weight, down_weight):
    micro_count, tok_dev, model_width = tokens.shape
    slot_count = tok_dev // 2
    rows_dev = micro_count * slot_count
    width_dev, hidden_dev = gate_weight.shape
    half = width_dev // 2
    n_x, n_z = SIZES["x"], SIZES["z"]

    select = slot_map(expert_ids, slot_count)

    def compact(values):
        own = jnp.sum(select[..., None] * values[:, None].astype(jnp.float32), axis=2)
        return own.astype(HALF).reshape(rows_dev, 2, 2, 2, half)

    scaled = (gates[..., None] * cotangent.astype(jnp.float32)).astype(HALF)
    own = jnp.stack([compact(tokens), compact(scaled)])
    own = jnp.transpose(own, (2, 4, 3, 0, 1, 5))[:, :, None]
    own = jnp.broadcast_to(own, (2, 2, n_x, 2, 2, rows_dev, half))
    got = lax.all_to_all(own.reshape(-1, 2, rows_dev, half), XY_GROUP, 0, 0)

    weight = jnp.concatenate([gate_weight, up_weight, down_weight.T], axis=1)
    weight = jnp.stack(picked(weight.reshape(2, half, 3 * hidden_dev), "y_lo"))
    maps = row_maps(n_x * n_z * 32)
    got, weight, maps = barrier((got, weight, maps))
    to_gathered, to_owners = maps
    weight = traded(weight)

    x_unit, c_unit = got[:, 0].reshape(-1, half), got[:, 1].reshape(-1, half)
    x_pieces = [x_unit, x_unit]
    for step in range(n_z // 2):
        x_pieces = x_pieces + next_round(x_pieces, step == n_z // 2 - 1)
    x_own = jnp.concatenate(x_pieces[1:], axis=0)
    x_own, c_unit, weight = barrier((x_own, c_unit, weight))
    gate_up = weight[:, :, : 2 * hidden_dev]

    x_other = shifted(x_own, "core", 1)
    partial = dot(x_own, gate_up[0], 1, 0) + dot(x_other, gate_up[1], 1, 0)
    c_pieces = next_round([c_unit, c_unit], False)
    partial, c_pieces = barrier((partial.astype(HALF), c_pieces))
    down = jnp.swapaxes(weight[:, :, 2 * hidden_dev :], 1, 2)

    acts = ring_sum(partial)
    c_pieces = [c_unit] + c_pieces
    for _ in range(n_z // 2 - 2):
        c_pieces = c_pieces + next_round(c_pieces, False)
    acts, c_pieces, down = barrier((acts, c_pieces, down))

    gate_act, up_act = acts[:, :hidden_dev], acts[:, hidden_dev:]
    sigma = jax.nn.sigmoid(gate_act)
    silu_act = gate_act * sigma
    slope = sigma * (1.0 + gate_act * (1.0 - sigma))
    hidden = jnp.concatenate(ring_join((silu_act * up_act).astype(HALF)), axis=0)
    c_pieces = c_pieces + next_round(c_pieces, True)
    hidden, c_pieces = barrier((hidden, c_pieces))
    c_own = jnp.concatenate(c_pieces, axis=0)

    placed = dot(to_owners, hidden, 1, 0).astype(HALF)
    out = shifted(dot(placed, down[1], 1, 0).astype(HALF), "core", 1)
    out = dot(placed, down[0], 1, 0) + out.astype(jnp.float32)
    c_other = shifted(c_own, "core", 1)
    back = dot(c_own, down[0], 1, 1) + dot(c_other, down[1], 1, 1)
    out, back = barrier((out.astype(HALF), back.astype(HALF)))

    out = send_home(out.reshape(n_x, -1, half), "x").astype(HALF)
    back_act = ring_sum(back)
    slopes = jnp.concatenate([back_act * up_act * slope, back_act * silu_act], axis=-1)
    slopes = ring_join(slopes.astype(HALF))
    early, hidden = barrier((slopes[2], hidden))
    slopes = jnp.concatenate(slopes[:2] + [early, slopes[3]], axis=0)
    hidden = dot(to_gathered, hidden, 1, 0).astype(HALF)
    down_pair = jnp.stack([dot(hidden, rows, 0, 0).astype(HALF) for rows in (c_own, c_other)])
    down_pair = traded(down_pair)
    slopes = dot(to_gathered, slopes, 1, 0).astype(HALF)
    pair = products((x_own, x_other), slopes)
    out, pair, down_pair = barrier((out, pair, down_pair))

    got = lax.all_to_all(out.reshape(-1, rows_dev, half), YZ_GROUP, 0, 0)
    pair = jnp.concatenate(picked(traded(pair), "y_lo"), axis=0)
    grad_gate = pair[:, :hidden_dev].astype(jnp.float32)
    grad_up = pair[:, hidden_dev:].astype(jnp.float32)
    got, grad_gate, grad_up = barrier((got, grad_gate, grad_up))
    got = jnp.sum(got.reshape(2, 2, n_z, 2, rows_dev, half).astype(jnp.float32), axis=2)
    grad_down = jnp.concatenate(picked(down_pair, "y_lo"), axis=1).astype(jnp.float32)
    slot_out = jnp.transpose(got, (3, 0, 2, 1, 4))
    slot_out = slot_out.reshape(micro_count, slot_count, 1, model_width)
    token_out = jnp.sum(select[..., None] * slot_out, axis=1)
    mixed = (gates[..., None] * token_out).astype(HALF)

    return (mixed, grad_gate, grad_up, grad_down)


def solution(mesh):
    fine = Mesh(mesh.devices.reshape(tuple(SIZES.values())), NAMES)
    tokens = DP + EXPERT
    return jax.shard_map(
        shards,
        mesh=fine,
        in_specs=(
            P(None, tokens, None),
            P(None, tokens, None),
            P(None, tokens, None),
            P(None, tokens),
            P(DP, EXPERT),
            P(DP, EXPERT),
            P(EXPERT, DP),
        ),
        out_specs=(
            P(None, tokens, None),
            P(DP, EXPERT),
            P(DP, EXPERT),
            P(EXPERT, DP),
        ),
        check_vma=False,
    )
```
